32 devices in a mesh: facet: 8 (over z, core), row: 2 (over y), sub: 2 (over x).
Axes of the slice: x: 2, y: 2, z: 4, core: 2. Of those that a mesh axis runs over, the one named last changes fastest.
Arguments:
- facet_model: bfloat16 [2, 4, 8192, 8192], P(None, 'sub', ('facet', 'row')), may hold values from -6 to 6
- sub_offsets: int32 [32], replicated, may hold values from 0 to 65535
- tile_rows: int32 [32, 4], P(('facet', 'row', 'sub')), may hold values from 0 to 120
- tile_counts: int32 [32], P(('facet', 'row', 'sub')), may hold values from 1 to 4, as said below
- visibilities: bfloat16 [32, 4, 32, 8, 256], P(('facet', 'row', 'sub')), may hold values from -6 to 6
Outputs:
- residual_facets: bfloat16 [2, 4, 8192, 8192], P(None, 'sub', ('facet', 'row'))
- residual_vis: bfloat16 [32, 4, 32, 8, 256], P(('facet', 'row', 'sub'))
The draws below stay inside these ranges and needn't reach their ends.
Inputs may be any that keep to these rules, and one draw needn't show every extreme that they name: tile_counts[s] tiles of subgrid s are live, the first ones; some subgrid has all 4 tiles live. Tile j of subgrid s covers subgrid rows tile_rows[s, j] to tile_rows[s, j] + 7; tiles may intersect.
All inputs are finite; a program needn't handle non-finite values.
Results may differ from the reference program's by a relative error of at most 0.014.
Values may be sent and summed in bfloat16 or wider, within the bound.
A program may use at most 192 MiB of HBM per device.

```python
import math
import jax
import jax.numpy as jnp
from jax import lax

SKY = 65536
FP = 8192
CS = 64
SG = 128
TMAX = 4
CH = 32
TR = 8
NF = 4
SUBGRIDS = 32


def draw_tile_counts(key, part):
    counts = jax.random.randint(key, (SUBGRIDS,), 1, TMAX + 1)
    chosen = jax.random.randint(jax.random.fold_in(key, 7), (), 0, SUBGRIDS)
    return jnp.where(jnp.arange(SUBGRIDS) == chosen, TMAX, counts).astype(jnp.int32)


def with_ends(array, key, least, high):
    shape = array.shape
    place = [jax.random.randint(jax.random.fold_in(key, axis), (), 0, shape[axis]) for axis in range(len(shape))]
    array = array.at[tuple(place)].set(least)
    longest = shape.index(max(shape))
    place[longest] = (place[longest] + 1) % shape[longest]
    return array.at[tuple(place)].set(high)


def block_levels(rng, extent, split, low, high):
    factor_of = 1.0
    for position, blocks in split:
        steps = jax.random.uniform(jax.random.fold_in(jax.random.fold_in(rng, 6), position), (blocks,), jnp.float32, low / len(split), high / len(split))
        factor_of = factor_of * jnp.repeat(jnp.exp(steps), extent[position] // blocks).reshape((-1,) + (1,) * (len(extent) - 1 - position))
    return factor_of


def normal_values(rng, dims, scale, reach, cuts=(), held_as=jnp.bfloat16):
    drawn = scale * jax.random.normal(rng, dims, jnp.float32)
    if cuts:
        drawn = drawn * block_levels(rng, dims, cuts, -0.22, 0.18)
    return jnp.clip(drawn, -reach, reach).astype(held_as)


def setup_inputs(seed: int = 0) -> dict:
    seeds = jax.random.split(jax.random.key(seed), 6)
    facet_model = normal_values(seeds[0], (2, NF, FP, FP), 1.0, 6.0, ((1, 2), (2, 16)))
    sub_offsets = with_ends(jax.random.randint(seeds[1], (SUBGRIDS,), 0, SKY), jax.random.fold_in(seeds[1], 1), 0, SKY - 1).astype(jnp.int32)
    tile_rows = with_ends(jax.random.randint(seeds[2], (SUBGRIDS, TMAX), 0, SG - TR + 1), jax.random.fold_in(seeds[2], 1), 0, SG - TR).astype(jnp.int32)
    tile_counts = draw_tile_counts(jax.random.fold_in(seeds[5], 71), 0)
    visibilities = normal_values(seeds[4], (SUBGRIDS, TMAX, CH, TR, 2 * SG), 1.0, 6.0, ((0, 32),))
    return {"facet_model": facet_model, "sub_offsets": sub_offsets, "tile_rows": tile_rows, "tile_counts": tile_counts, "visibilities": visibilities}


two_pi = 2.0 * math.pi

def modmul(left, right, modulus):
    lower = right % 256
    upper = right // 256
    return (left * lower % modulus + left * upper % modulus * 256) % modulus

def window_taper(pixels):
    places = jnp.arange(pixels, dtype=jnp.float32)
    curve = jnp.sin(math.pi * (places + 0.5) / pixels)
    return 0.25 + 0.75 * curve * curve

def turn_pair(phase_index, modulus):
    angle = phase_index.astype(jnp.float32) * (-two_pi / modulus)
    return (jnp.cos(angle), jnp.sin(angle))

def column_table(facet_ids, pixels, width, modulus, ratio):
    spacing = modulus // pixels
    column_pos = facet_ids // ratio % ratio * pixels
    freqs = spacing * jnp.arange(width, dtype=jnp.int32)
    places = (column_pos[:, None] + jnp.arange(pixels, dtype=jnp.int32)[None, :]) % modulus
    cosine, sine = turn_pair(modmul(freqs[None, :, None], places[:, None, :], modulus), modulus)
    scaled = window_taper(pixels) / math.sqrt(pixels)
    return (jnp.stack([cosine, sine], axis=1) * scaled).astype(jnp.bfloat16)

def row_table(offsets, pixels, width, modulus):
    spacing = modulus // pixels
    freqs = (offsets[:, None] + spacing * jnp.arange(width, dtype=jnp.int32)[None, :]) % modulus
    places = jnp.arange(pixels, dtype=jnp.int32)
    cosine, sine = turn_pair(modmul(freqs[:, :, None], places[None, None, :], modulus), modulus)
    scaled = window_taper(pixels) / math.sqrt(pixels)
    return ((jnp.stack([cosine, sine], axis=1) * scaled).astype(jnp.bfloat16), freqs)

def facet_turn(freqs, facet_ids, modulus, pixels, ratio):
    row_pos = facet_ids % ratio * pixels
    return turn_pair(modmul(freqs[:, :, None], row_pos[None, None, :], modulus), modulus)

def grid_table(size):
    places = jnp.arange(size, dtype=jnp.int32)
    angle = (places[:, None] * places[None, :] % size).astype(jnp.float32) * (two_pi / size)
    return (jnp.stack([jnp.cos(angle), jnp.sin(angle)]) / math.sqrt(size)).astype(jnp.bfloat16)

def slot_table(count, ratio):
    facet_ids = jnp.arange(count, dtype=jnp.int32)
    first = facet_ids % ratio
    second = facet_ids // ratio % ratio
    options = jnp.arange(ratio, dtype=jnp.int32)
    hits = (first[:, None, None] == options[None, :, None]) & (second[:, None, None] == options[None, None, :])
    return hits.astype(jnp.bfloat16)

def as_float(value):
    return value.astype(jnp.float32)

def finish_contrib(raw, turn_real, turn_imag):
    part_real = raw[:, 0, :, :, :, 0] - raw[:, 1, :, :, :, 1]
    part_imag = raw[:, 0, :, :, :, 1] + raw[:, 1, :, :, :, 0]
    real_turn = turn_real[:, :, :, None, None]
    imag_turn = turn_imag[:, :, :, None, None]
    out_real = real_turn * part_real - imag_turn * part_imag
    out_imag = real_turn * part_imag + imag_turn * part_real
    joined = jnp.stack([out_real, out_imag], axis=4)
    return jnp.transpose(joined, (0, 2, 3, 1, 4, 5)).astype(jnp.bfloat16)

def assemble(contrib, slots, grid):
    width = contrib.shape[2]
    terms = contrib.shape[1]
    ratio = slots.shape[1]
    size = width * ratio
    placed = jnp.einsum('fab,ftkcl->katclb', as_float(slots), as_float(contrib))
    amatrix = placed.reshape(size, terms, 2, size).astype(jnp.bfloat16)
    first = jnp.einsum('zum,mtcn->zutcn', as_float(grid), as_float(amatrix))
    front = jnp.stack([first[0, :, :, 0] - first[1, :, :, 1], first[0, :, :, 1] + first[1, :, :, 0]], axis=2).astype(jnp.bfloat16)
    second = jnp.einsum('utcn,zvn->utczv', as_float(front), as_float(grid))
    sky_real = second[:, :, 0, 0] - second[:, :, 1, 1]
    sky_imag = second[:, :, 0, 1] + second[:, :, 1, 0]
    return jnp.stack([sky_real, sky_imag], axis=2).astype(jnp.bfloat16)

def degrid_grid(sky_grid, rows, count, observed):
    slots_count, channels, tile_height, span = observed.shape
    size = sky_grid.shape[0]
    nu_values = (jnp.arange(channels, dtype=jnp.float32) + 0.5) / channels - 0.5
    live = jnp.arange(slots_count, dtype=jnp.int32) < count
    target = rows[:, None] + jnp.arange(tile_height, dtype=jnp.int32)[None, :]
    hits = (target[:, :, None] == jnp.arange(size, dtype=jnp.int32)[None, None, :]) & live[:, None, None]
    placer = hits.astype(jnp.bfloat16).reshape(slots_count * tile_height, size)
    model_rows = jnp.dot(placer, sky_grid.reshape(size, 2 * span), preferred_element_type=jnp.float32)
    model_rows = model_rows.reshape(slots_count, tile_height, 2, span)
    model = model_rows[:, None, :, 0] + nu_values[None, :, None, None] * model_rows[:, None, :, 1]
    residual = (observed.astype(jnp.float32) - model) * live[:, None, None, None].astype(jnp.float32)
    weighted = jnp.stack([lax.optimization_barrier(jnp.sum(residual, axis=1)), lax.optimization_barrier(jnp.sum(nu_values[None, :, None, None] * residual, axis=1))], axis=2)
    weighted = weighted.astype(jnp.bfloat16).reshape(slots_count * tile_height, 2 * span)
    regrid = lax.dot_general(placer, weighted, (((0,), (0,)), ((), ())), preferred_element_type=jnp.float32)
    return (residual.astype(jnp.bfloat16), regrid.reshape(size, 2, 2, size).astype(jnp.bfloat16))

def adjoint_grid(regrid, grid):
    first = jnp.einsum('zum,utcv->zmtcv', as_float(grid), as_float(regrid))
    back_real = first[0, :, :, 0] + first[1, :, :, 1]
    back_imag = first[0, :, :, 1] - first[1, :, :, 0]
    back_front = jnp.stack([back_real, back_imag], axis=2).astype(jnp.bfloat16)
    second = jnp.einsum('mtcv,zvn->mtczn', as_float(back_front), as_float(grid))
    grid_real = second[:, :, 0, 0] + second[:, :, 1, 1]
    grid_imag = second[:, :, 1, 0] - second[:, :, 0, 1]
    return jnp.stack([grid_real, grid_imag], axis=2).astype(jnp.bfloat16)

def select_slots(back_grid, slots):
    ratio = slots.shape[1]
    size = back_grid.shape[0]
    width = size // ratio
    terms = back_grid.shape[1]
    shaped = back_grid.reshape(width, ratio, terms, 2, width, ratio)
    return jnp.einsum('fab,katclb->ftkcl', as_float(slots), as_float(shaped)).astype(jnp.bfloat16)

def turn_back(returned, turn_real, turn_imag):
    real_turn = jnp.transpose(turn_real, (0, 2, 1))[:, :, None, :, None]
    imag_turn = jnp.transpose(turn_imag, (0, 2, 1))[:, :, None, :, None]
    part_real = returned[:, :, :, :, 0].astype(jnp.float32)
    part_imag = returned[:, :, :, :, 1].astype(jnp.float32)
    turned = jnp.stack([real_turn * part_real + imag_turn * part_imag, real_turn * part_imag - imag_turn * part_real], axis=4)
    return turned.astype(jnp.bfloat16)

def paired_terms(turned):
    real_part = turned[:, :, :, :, 0]
    imag_part = turned[:, :, :, :, 1]
    pair_real = jnp.stack([real_part, imag_part], axis=1)
    pair_imag = jnp.stack([imag_part, -real_part], axis=1)
    return jnp.stack([pair_real, pair_imag], axis=5)

def strip_terms(table_part, turned):
    return jnp.einsum('szkp,szftkcl->pftcl', as_float(table_part), as_float(paired_terms(turned)))

def reference(facet_model, sub_offsets, tile_rows, tile_counts, visibilities):
    ratio = SG // CS
    facet_ids = jnp.arange(NF, dtype=jnp.int32)
    columns = column_table(facet_ids, FP, CS, SKY, ratio)
    strips = jnp.einsum('tfpq,fckq->pftck', as_float(facet_model), as_float(columns)).astype(jnp.bfloat16)
    slots = slot_table(NF, ratio)
    grid = grid_table(SG)

    def one_subgrid(carry, inputs):
        offset, rows, count, observed = inputs
        rtable, freqs = row_table(offset[None], FP, CS, SKY)
        turn_real, turn_imag = facet_turn(freqs, facet_ids, SKY, FP, ratio)
        raw = jnp.einsum('szkp,pftcl->szkftcl', as_float(rtable), as_float(strips))
        contrib = finish_contrib(raw, turn_real, turn_imag)[0]
        sky_grid = assemble(contrib, slots, grid)
        residual, regrid = degrid_grid(sky_grid, rows, count, observed)
        back_grid = adjoint_grid(regrid, grid)
        returned = select_slots(back_grid, slots)[None]
        turned = turn_back(returned, turn_real, turn_imag)
        return (carry + strip_terms(rtable, turned), residual)
    start = jnp.zeros((FP, NF, 2, 2, CS), jnp.float32)
    strip_sum, residual_vis = lax.scan(one_subgrid, start, (sub_offsets, tile_rows, tile_counts, visibilities))
    strip_round = strip_sum.astype(jnp.bfloat16)
    residual_facets = jnp.einsum('pftck,fckq->tfpq', as_float(strip_round), as_float(columns)).astype(jnp.bfloat16)
    return (residual_facets, residual_vis)
```

```python
import functools
import math

import jax
import jax.numpy as jnp
from jax import lax
from jax.experimental import pallas as pl
from jax.experimental.pallas import tpu as pltpu
from jax.sharding import PartitionSpec as P

SKY = 65536
CS = 64
SG = 128
TERMS = 2

two_pi = 2.0 * math.pi
F32 = jnp.float32
BF16 = jnp.bfloat16


def unit(phase, modulus, sign=-1.0):
    angle = phase.astype(F32) * (sign * two_pi / modulus)
    return jnp.cos(angle), jnp.sin(angle)


def taper_of(places, pixels):
    curve = jnp.sin(math.pi * (places.astype(F32) + 0.5) / pixels)
    return (0.25 + 0.75 * curve * curve) / math.sqrt(pixels)


def iota(count):
    return jnp.arange(count, dtype=jnp.int32)


def column_table(pixels):
    spacing = SKY // pixels
    freqs = spacing * iota(CS)
    lane = 128
    low = unit(freqs[:, None] * iota(lane)[None, :] % SKY, SKY)
    high = unit(freqs[:, None] * (lane * iota(pixels // lane))[None, :] % SKY, SKY)
    scale = taper_of(iota(pixels), pixels).reshape(pixels // lane, lane)
    lr, li, hr, hi, scale = lax.optimization_barrier((*low, *high, scale))
    lr, li, hr, hi = lr[:, None, :], li[:, None, :], hr[:, :, None], hi[:, :, None]
    real = (hr * lr - hi * li) * scale
    imag = (hr * li + hi * lr) * scale
    return jnp.concatenate([real, imag], axis=0).astype(BF16).reshape(2 * CS, pixels)


def row_table(offsets, pixels, first_row, count):
    spacing = SKY // pixels
    places = first_row + iota(count)
    base = unit(offsets[:, None] * places[None, :] % SKY, SKY)
    step = unit(spacing * iota(CS)[:, None] * places[None, :] % SKY, SKY)
    scale = taper_of(places, pixels)
    br, bi, sr, si = lax.optimization_barrier((*base, step[0] * scale, step[1] * scale))
    br, bi, sr, si = br[:, None, :], bi[:, None, :], sr[None], si[None]
    real = br * sr - bi * si
    imag = br * si + bi * sr
    return real.astype(BF16), imag.astype(BF16)


def grid_tables():
    ratio = SG // CS
    order = (ratio * iota(CS)[None, :] + iota(ratio)[:, None]).reshape(SG)
    cosine, sine = unit(iota(SG)[:, None] * order[None, :] % SG, SG, 1.0)
    real = (cosine / math.sqrt(SG)).astype(BF16)
    imag = (sine / math.sqrt(SG)).astype(BF16)
    left = jnp.concatenate([real, imag], axis=1)
    back = jnp.concatenate([real.T, imag.T], axis=1)
    tr = real.T.reshape(ratio, CS, SG)
    ti = imag.T.reshape(ratio, CS, SG)
    right = jnp.stack(
        [jnp.concatenate([tr, ti], axis=2), jnp.concatenate([-ti, tr], axis=2)], axis=1
    ).reshape(2 * SG, 2 * SG)
    return left, back, right, right.T


def times_i(value):
    half = value.shape[-1] // 2
    return jnp.concatenate([-value[..., half:], value[..., :half]], axis=-1)


def dot(left, right):
    return jnp.dot(left, right, preferred_element_type=F32)


def subgrid_cycle(offset_mod, spacing, rows, count, contrib, left, back, right, right_t, observe, emit):
    ratio = SG // CS
    slot = lax.broadcasted_iota(jnp.int32, (SG, 1), 0) // CS
    angle = (offset_mod * slot % spacing).astype(F32) * (-two_pi / spacing)
    turn_r, turn_i = jnp.cos(angle), jnp.sin(angle)
    fronts = []
    for t in range(TERMS):
        parts = []
        for b in range(ratio):
            raw = contrib(t, b)
            placed = (turn_r * raw + turn_i * times_i(raw)).astype(BF16)
            parts.append(jnp.concatenate([placed, times_i(placed)], axis=0))
        fronts.append(dot(left, jnp.concatenate(parts, axis=1)).astype(BF16))
    sky = [dot(front, right).astype(BF16) for front in fronts]
    tiles = len(rows)
    height = 8
    group = tiles * height
    line = lax.broadcasted_iota(jnp.int32, (group, 1), 0)
    target = jnp.zeros((group, 1), jnp.int32)
    for j in range(tiles):
        target = jnp.where(line // height == j, rows[j] + line - j * height, target)
    live = line // height < count
    column = lax.broadcasted_iota(jnp.int32, (group, SG), 1)
    placer = jnp.where((target == column) & live, 1.0, 0.0).astype(BF16)
    model = [dot(placer, term) for term in sky]
    live_f = live.astype(F32)
    sums = [[], []]
    for j in range(tiles):
        part = slice(j * height, (j + 1) * height)
        sums_j = observe(j, model[0][part], model[1][part], live_f[part])
        sums[0].append(sums_j[0])
        sums[1].append(sums_j[1])
    out = []
    for t in range(TERMS):
        weighted = jnp.concatenate(sums[t], axis=0).astype(BF16)
        regrid = lax.dot_general(
            placer, weighted, (((0,), (0,)), ((), ())), preferred_element_type=F32
        ).astype(BF16)
        front = dot(back, jnp.concatenate([regrid, -times_i(regrid)], axis=0)).astype(BF16)
        grid = dot(front, right_t).astype(BF16).astype(F32)
        out.append([])
        for b in range(ratio):
            part = grid[:, b * SG : (b + 1) * SG]
            out[t].append((turn_r * part - turn_i * times_i(part)).astype(BF16))
    return out


def observe_tile(vis_ref, res_ref, j, first, second, live):
    channels = vis_ref.shape[1]
    sum0 = jnp.zeros(first.shape, F32)
    sum1 = jnp.zeros(first.shape, F32)
    for c in range(channels):
        nu = (c + 0.5) / channels - 0.5
        residual = (vis_ref[j, c].astype(F32) - (first + nu * second)) * live
        res_ref[j, c] = residual.astype(BF16)
        sum0 += residual
        sum1 += nu * residual
    return sum0, sum1


def cycle_kernel(spacing, scal_ref, x_ref, left_ref, back_ref, right_ref, right_t_ref, vis_ref, y_ref, res_ref):
    tiles = vis_ref.shape[0]
    rows = [scal_ref[2 + j] for j in range(tiles)]
    out = subgrid_cycle(
        scal_ref[0], spacing, rows, scal_ref[1],
        lambda t, b: x_ref[t, b].astype(F32),
        left_ref[...], back_ref[...], right_ref[...], right_t_ref[...],
        functools.partial(observe_tile, vis_ref, res_ref), None,
    )
    for t in range(TERMS):
        for b in range(SG // CS):
            y_ref[t, b] = out[t][b]


def local(facet_model, sub_offsets, tile_rows, tile_counts, visibilities):
    terms, facets, rows_here, pixels = facet_model.shape
    spacing = SKY // pixels
    ratio = SG // CS
    pairs = lax.axis_size("sub")
    pair = lax.axis_index("sub")
    strip_group = lax.axis_index(("facet", "row"))
    owner = strip_group * pairs + pair
    columns = column_table(pixels)
    real, imag = row_table(sub_offsets, pixels, strip_group * rows_here, rows_here)
    table = jnp.stack([real, imag], axis=2)
    strips = jnp.einsum(
        "tfpq,nq->tfpn", facet_model, columns, preferred_element_type=F32
    ).astype(BF16)
    both = jnp.stack([strips, times_i(strips)], axis=2)
    partial = jnp.einsum("skzp,tfzpn->tfskn", table, both, preferred_element_type=F32).astype(BF16)
    summed = lax.psum_scatter(partial, ("facet", "row"), scatter_dimension=2, tiled=True)
    contrib = lax.all_to_all(summed, "sub", split_axis=2, concat_axis=1, tiled=True)
    contrib = contrib.reshape(terms, ratio, SG, 2 * CS)
    left, back, right, right_t = grid_tables()
    scal = jnp.concatenate(
        [lax.dynamic_slice(sub_offsets, (owner,), (1,)) % spacing, tile_counts, tile_rows[0]]
    )
    vmem = pl.BlockSpec(memory_space=pltpu.VMEM)
    returned, residual = pl.pallas_call(
        functools.partial(cycle_kernel, spacing),
        out_shape=(
            jax.ShapeDtypeStruct(contrib.shape, BF16),
            jax.ShapeDtypeStruct(visibilities.shape[1:], BF16),
        ),
        in_specs=[pl.BlockSpec(memory_space=pltpu.SMEM)] + [vmem] * 6,
        out_specs=(vmem, vmem),
        compiler_params=pltpu.CompilerParams(vmem_limit_bytes=32 * 2**20),
    )(scal, contrib, left, back, right, right_t, visibilities[0])
    returned = returned.reshape(terms, facets * pairs, 1, CS, 2 * CS)
    received = lax.all_to_all(returned, "sub", split_axis=1, concat_axis=2, tiled=True)
    turned = lax.all_gather(received, ("facet", "row"), axis=2, tiled=True)
    pairs_of = jnp.stack([turned, -times_i(turned)], axis=4)
    strip_round = jnp.einsum(
        "skzp,tfskzn->tfpn", table, pairs_of, preferred_element_type=F32
    ).astype(BF16)
    residual_facets = jnp.einsum(
        "tfpn,nq->tfpq", strip_round, columns, preferred_element_type=F32
    ).astype(BF16)
    return (residual_facets, residual[None])


def solution(mesh):
    placed = (
        P(None, "sub", ("facet", "row"), None),
        P(),
        P(("facet", "row", "sub"), None),
        P(("facet", "row", "sub")),
        P(("facet", "row", "sub"), None, None, None, None),
    )
    return jax.shard_map(
        local,
        mesh=mesh,
        in_specs=placed,
        out_specs=(
            P(None, "sub", ("facet", "row"), None),
            P(("facet", "row", "sub"), None, None, None, None),
        ),
        check_vma=False,
    )
```

```python
import functools
import math

import jax
import jax.numpy as jnp
from jax import lax
from jax.experimental import pallas as pl
from jax.experimental.pallas import tpu as pltpu
from jax.sharding import PartitionSpec as P

SKY = 65536
CS = 64
SG = 128
TERMS = 2

two_pi = 2.0 * math.pi
F32 = jnp.float32
BF16 = jnp.bfloat16


def unit(phase, modulus, sign=-1.0):
    angle = phase.astype(F32) * (sign * two_pi / modulus)
    return jnp.cos(angle), jnp.sin(angle)


def taper_of(places, pixels):
    curve = jnp.sin(math.pi * (places.astype(F32) + 0.5) / pixels)
    return (0.25 + 0.75 * curve * curve) / math.sqrt(pixels)


def iota(count):
    return jnp.arange(count, dtype=jnp.int32)


def column_table(pixels):
    spacing = SKY // pixels
    freqs = spacing * iota(CS)
    lane = 128
    low = unit(freqs[:, None] * iota(lane)[None, :] % SKY, SKY)
    high = unit(freqs[:, None] * (lane * iota(pixels // lane))[None, :] % SKY, SKY)
    scale = taper_of(iota(pixels), pixels).reshape(pixels // lane, lane)
    lr, li, hr, hi, scale = lax.optimization_barrier((*low, *high, scale))
    lr, li, hr, hi = lr[:, None, :], li[:, None, :], hr[:, :, None], hi[:, :, None]
    real = (hr * lr - hi * li) * scale
    imag = (hr * li + hi * lr) * scale
    return jnp.concatenate([real, imag], axis=0).astype(BF16).reshape(2 * CS, pixels)


def row_table(offsets, pixels, first_row, count):
    spacing = SKY // pixels
    places = first_row + iota(count)
    base = unit(offsets[:, None] * places[None, :] % SKY, SKY)
    step = unit(spacing * iota(CS)[:, None] * places[None, :] % SKY, SKY)
    scale = taper_of(places, pixels)
    br, bi, sr, si = lax.optimization_barrier((*base, step[0] * scale, step[1] * scale))
    br, bi, sr, si = br[:, None, :], bi[:, None, :], sr[None], si[None]
    real = br * sr - bi * si
    imag = br * si + bi * sr
    return real.astype(BF16), imag.astype(BF16)


def grid_tables():
    ratio = SG // CS
    order = (ratio * iota(CS)[None, :] + iota(ratio)[:, None]).reshape(SG)
    cosine, sine = unit(iota(SG)[:, None] * order[None, :] % SG, SG, 1.0)
    real = (cosine / math.sqrt(SG)).astype(BF16)
    imag = (sine / math.sqrt(SG)).astype(BF16)
    left = jnp.concatenate([real, imag], axis=1)
    back = jnp.concatenate([real.T, imag.T], axis=1)
    tr = real.T.reshape(ratio, CS, SG)
    ti = imag.T.reshape(ratio, CS, SG)
    right = jnp.stack(
        [jnp.concatenate([tr, ti], axis=2), jnp.concatenate([-ti, tr], axis=2)], axis=1
    ).reshape(2 * SG, 2 * SG)
    return left, back, right, right.T


def times_i(value):
    half = value.shape[-1] // 2
    return jnp.concatenate([-value[..., half:], value[..., :half]], axis=-1)


def dot(left, right):
    return jnp.dot(left, right, preferred_element_type=F32)


def subgrid_cycle(offset_mod, spacing, rows, count, contrib, left, back, right, right_t, observe, emit):
    ratio = SG // CS
    slot = lax.broadcasted_iota(jnp.int32, (SG, 1), 0) // CS
    angle = (offset_mod * slot % spacing).astype(F32) * (-two_pi / spacing)
    turn_r, turn_i = jnp.cos(angle), jnp.sin(angle)
    fronts = []
    for t in range(TERMS):
        parts = []
        for b in range(ratio):
            raw = contrib(t, b)
            placed = (turn_r * raw + turn_i * times_i(raw)).astype(BF16)
            parts.append(jnp.concatenate([placed, times_i(placed)], axis=0))
        fronts.append(dot(left, jnp.concatenate(parts, axis=1)).astype(BF16))
    sky = [dot(front, right).astype(BF16) for front in fronts]
    tiles = len(rows)
    height = 8
    group = tiles * height
    line = lax.broadcasted_iota(jnp.int32, (group, 1), 0)
    target = jnp.zeros((group, 1), jnp.int32)
    for j in range(tiles):
        target = jnp.where(line // height == j, rows[j] + line - j * height, target)
    live = line // height < count
    column = lax.broadcasted_iota(jnp.int32, (group, SG), 1)
    placer = jnp.where((target == column) & live, 1.0, 0.0).astype(BF16)
    model = [dot(placer, term) for term in sky]
    live_f = live.astype(F32)
    sums = [[], []]
    for j in range(tiles):
        part = slice(j * height, (j + 1) * height)
        sums_j = observe(j, model[0][part], model[1][part], live_f[part])
        sums[0].append(sums_j[0])
        sums[1].append(sums_j[1])
    out = []
    for t in range(TERMS):
        weighted = jnp.concatenate(sums[t], axis=0).astype(BF16)
        regrid = lax.dot_general(
            placer, weighted, (((0,), (0,)), ((), ())), preferred_element_type=F32
        ).astype(BF16)
        front = dot(back, jnp.concatenate([regrid, -times_i(regrid)], axis=0)).astype(BF16)
        grid = dot(front, right_t).astype(BF16).astype(F32)
        out.append([])
        for b in range(ratio):
            part = grid[:, b * SG : (b + 1) * SG]
            out[t].append((turn_r * part - turn_i * times_i(part)).astype(BF16))
    return out


def observe_tile(vis_ref, res_ref, j, first, second, live):
    channels = vis_ref.shape[1]
    sum0 = jnp.zeros(first.shape, F32)
    sum1 = jnp.zeros(first.shape, F32)
    for c in range(channels):
        nu = (c + 0.5) / channels - 0.5
        residual = (vis_ref[j, c].astype(F32) - (first + nu * second)) * live
        res_ref[j, c] = residual.astype(BF16)
        sum0 += residual
        sum1 += nu * residual
    return sum0, sum1


def cycle_kernel(
    spacing, scal_ref, x_ref, left_ref, back_ref, right_ref, right_t_ref, vis_ref,
    g_ref, res_ref,
    core_sum, row_recv, row_sum, z_recv, full, turned, send, recv,
):
    chunks, cores, rows, depth = x_ref.shape[:4]
    pairs = full.shape[1]
    ratio = SG // CS
    facet, row, sub = lax.axis_index("facet"), lax.axis_index("row"), lax.axis_index("sub")
    core, z = lax.rem(facet, cores), facet // cores
    other = {"facet": facet + 1 - 2 * core}

    def row_peer(d):
        return {"row": lax.rem(row + d, rows)}

    def z_place(d):
        return lax.rem(z + d, depth)

    def z_peer(d):
        return {"facet": z_place(d) * cores + core}

    def sub_place(d):
        return lax.rem(sub + d, pairs)

    def sub_peer(d):
        return {"sub": sub_place(d)}

    peers = [other]
    peers += [row_peer(d) for d in range(1, rows)]
    peers += [z_peer(d) for d in range(1, depth)]
    peers += [sub_peer(d) for d in range(1, pairs)]
    barrier = pltpu.get_barrier_semaphore()
    for peer in peers:
        pl.semaphore_signal(barrier, inc=1, device_id=peer, device_id_type=pl.DeviceIdType.MESH)
    pl.semaphore_wait(barrier, len(peers))

    row_at, z_at, sub_at = 1, rows, rows + depth - 1
    started = []

    def send_to(way, chunk, slot, source, target, peer):
        copy = pltpu.make_async_remote_copy(
            src_ref=source,
            dst_ref=target,
            send_sem=send.at[way, chunk, slot],
            recv_sem=recv.at[way, chunk, slot],
            device_id=peer,
            device_id_type=pl.DeviceIdType.MESH,
        )
        copy.start()
        started.append(copy)
        return copy

    def core_start(c):
        return [send_to(0, c, 0, x_ref.at[c, 1 - core], core_sum.at[c], other)]

    def row_start(c):
        @pl.loop(0, rows * depth)
        def _(i):
            r, p = i // depth, lax.rem(i, depth)
            total = core_sum[c, r, p].astype(F32) + x_ref[c, core, r, p].astype(F32)
            core_sum[c, r, p] = total.astype(BF16)

        return [
            send_to(
                0, c, row_at + d - 1,
                core_sum.at[c, lax.rem(row + d, rows)], row_recv.at[c, d - 1], row_peer(d),
            )
            for d in range(1, rows)
        ]

    def z_start(c):
        @pl.loop(0, depth)
        def _(p):
            total = core_sum[c, row, p].astype(F32)
            for d in range(1, rows):
                total += row_recv[c, d - 1, p].astype(F32)
            row_sum[c, p] = total.astype(BF16)

        return [
            send_to(
                0, c, z_at + d - 1, row_sum.at[c, z_place(d)], z_recv.at[c, d - 1], z_peer(d)
            )
            for d in range(1, depth)
        ]

    def sub_start(c):
        total = row_sum[c, z].astype(F32)
        for d in range(1, depth):
            total += z_recv[c, d - 1].astype(F32)
        z_recv[c, 0] = total.astype(BF16)
        full[c, sub] = z_recv[c, 0, pl.ds(pl.multiple_of(sub * CS, CS), CS)]
        return [
            send_to(
                0, c, sub_at + d - 1,
                z_recv.at[c, 0, pl.ds(pl.multiple_of(sub_place(d) * CS, CS), CS)],
                full.at[c, sub], sub_peer(d),
            )
            for d in range(1, pairs)
        ]

    def wait(copies):
        for copy in copies:
            copy.wait_recv()

    def run(stages):
        flying = [[None] * chunks for _ in stages]
        for c in range(chunks):
            flying[0][c] = stages[0](c)
        for step in range(chunks + len(stages) - 2):
            for level in range(len(stages) - 1, 0, -1):
                c = step - (level - 1)
                if 0 <= c < chunks:
                    wait(flying[level - 1][c])
                    flying[level][c] = stages[level](c)
        for c in range(chunks):
            wait(flying[-1][c])

    run([core_start, row_start, z_start, sub_start])

    tiles = vis_ref.shape[0]

    def contrib(t, b):
        return jnp.concatenate(
            [full[t * ratio + a, b].astype(F32) for a in range(ratio)], axis=0
        )

    out = subgrid_cycle(
        scal_ref[0], spacing, [scal_ref[2 + j] for j in range(tiles)], scal_ref[1], contrib,
        left_ref[...], back_ref[...], right_ref[...], right_t_ref[...],
        functools.partial(observe_tile, vis_ref, res_ref), None,
    )
    for t in range(TERMS):
        for b in range(ratio):
            for a in range(ratio):
                turned[t * ratio + a, b] = out[t][b][a * CS : (a + 1) * CS]

    def mine(c):
        return g_ref.at[c, core, row, z, pl.ds(pl.multiple_of(sub * CS, CS), CS)]

    def back_sub(c):
        g_ref[c, core, row, z, pl.ds(pl.multiple_of(sub * CS, CS), CS)] = turned[c, sub]
        return [
            send_to(1, c, sub_at + d - 1, turned.at[c, sub_place(d)], mine(c), sub_peer(d))
            for d in range(1, pairs)
        ]

    def back_z(c):
        return [
            send_to(
                1, c, z_at + d - 1,
                g_ref.at[c, core, row, z], g_ref.at[c, core, row, z], z_peer(d),
            )
            for d in range(1, depth)
        ]

    def back_row(c):
        return [
            send_to(
                1, c, row_at + d - 1, g_ref.at[c, core, row], g_ref.at[c, core, row], row_peer(d)
            )
            for d in range(1, rows)
        ]

    def back_core(c):
        return [send_to(1, c, 0, g_ref.at[c, core], g_ref.at[c, core], other)]

    run([back_sub, back_z, back_row, back_core])
    for copy in started:
        copy.wait_send()


def exchange(partial, scal, tables, observed, spacing):
    chunks, cores, rows, depth, span, lanes = partial.shape
    pairs = span // CS
    vmem = pl.BlockSpec(memory_space=pltpu.VMEM)
    slots = rows + depth + pairs - 2
    return pl.pallas_call(
        functools.partial(cycle_kernel, spacing),
        out_shape=(
            jax.ShapeDtypeStruct(partial.shape, BF16),
            jax.ShapeDtypeStruct(observed.shape, BF16),
        ),
        in_specs=[pl.BlockSpec(memory_space=pltpu.SMEM)] + [vmem] * 6,
        out_specs=(vmem, vmem),
        scratch_shapes=[
            pltpu.VMEM((chunks, rows, depth, span, lanes), BF16),
            pltpu.VMEM((chunks, rows - 1, depth, span, lanes), BF16),
            pltpu.VMEM((chunks, depth, span, lanes), BF16),
            pltpu.VMEM((chunks, depth - 1, span, lanes), BF16),
            pltpu.VMEM((chunks, pairs, CS, lanes), BF16),
            pltpu.VMEM((chunks, pairs, CS, lanes), BF16),
            pltpu.SemaphoreType.DMA((2, chunks, slots)),
            pltpu.SemaphoreType.DMA((2, chunks, slots)),
        ],
        compiler_params=pltpu.CompilerParams(
            collective_id=0, has_side_effects=True, vmem_limit_bytes=56 * 2**20
        ),
    )(scal, partial, *tables, observed)


def local(facet_model, sub_offsets, tile_rows, tile_counts, visibilities):
    terms, facets, rows_here, pixels = facet_model.shape
    spacing = SKY // pixels
    rows, pairs = lax.axis_size("row"), lax.axis_size("sub")
    cores = 2
    depth = lax.axis_size("facet") // cores
    strip_group = lax.axis_index(("facet", "row"))
    owner = strip_group * pairs + lax.axis_index("sub")
    columns = column_table(pixels)
    offsets = sub_offsets.reshape(depth, cores, rows, pairs).transpose(1, 2, 0, 3).reshape(-1)
    real, imag = row_table(offsets, pixels, strip_group * rows_here, rows_here)
    table = jnp.stack([real, imag], axis=2)
    strips = jnp.einsum(
        "tfpq,nq->tfpn", facet_model, columns, preferred_element_type=F32
    ).astype(BF16)
    both = jnp.stack([strips, times_i(strips)], axis=2)
    partial = jnp.einsum("skzp,tfzpn->tfskn", table, both, preferred_element_type=F32).astype(BF16)
    partial = partial.reshape(terms * facets, cores, rows, depth, pairs * CS, 2 * CS)
    scal = jnp.concatenate(
        [lax.dynamic_slice(sub_offsets, (owner,), (1,)) % spacing, tile_counts, tile_rows[0]]
    )
    turned, residual = exchange(partial, scal, grid_tables(), visibilities[0], spacing)
    turned = turned.reshape(terms, facets, sub_offsets.shape[0], CS, 2 * CS)
    pairs_of = jnp.stack([turned, -times_i(turned)], axis=4)
    strip_round = jnp.einsum(
        "skzp,tfskzn->tfpn", table, pairs_of, preferred_element_type=F32
    ).astype(BF16)
    residual_facets = jnp.einsum(
        "tfpn,nq->tfpq", strip_round, columns, preferred_element_type=F32
    ).astype(BF16)
    return (residual_facets, residual[None])


def solution(mesh):
    placed = (
        P(None, "sub", ("facet", "row"), None),
        P(),
        P(("facet", "row", "sub"), None),
        P(("facet", "row", "sub")),
        P(("facet", "row", "sub"), None, None, None, None),
    )
    return jax.shard_map(
        local,
        mesh=mesh,
        in_specs=placed,
        out_specs=(
            P(None, "sub", ("facet", "row"), None),
            P(("facet", "row", "sub"), None, None, None, None),
        ),
        check_vma=False,
    )
```

```python
import functools
import math

import jax
import jax.numpy as jnp
from jax import lax
from jax.experimental import pallas as pl
from jax.experimental.pallas import tpu as pltpu
from jax.sharding import PartitionSpec as P

SKY = 65536
CS = 64
SG = 128
TERMS = 2
VMEM_LIMIT = 62 * 2**20

two_pi = 2.0 * math.pi
F32 = jnp.float32
BF16 = jnp.bfloat16


def unit(phase, modulus, sign=-1.0):
    angle = phase.astype(F32) * (sign * two_pi / modulus)
    return jnp.cos(angle), jnp.sin(angle)


def iota(count):
    return jnp.arange(count, dtype=jnp.int32)


def along(shape, axis):
    return lax.broadcasted_iota(jnp.int32, shape, axis)


def fill_columns(cols_ref, high_r, high_i, high_c, high_s):
    pixels, lanes = cols_ref.shape
    spacing = SKY // pixels
    block = 128
    count = pixels // block
    freq = spacing * lax.rem(along((count, lanes), 1), CS)
    high_r[...], high_i[...] = unit(freq * (block * along((count, lanes), 0)) % SKY, SKY)
    step = block * along((count, lanes), 0).astype(F32) * (two_pi / pixels)
    high_c[...], high_s[...] = jnp.cos(step), jnp.sin(step)
    shape = (block, lanes)
    low_r, low_i = unit(spacing * lax.rem(along(shape, 1), CS) * along(shape, 0) % SKY, SKY)
    first = along(shape, 1) < CS
    low = jnp.where(first, low_r, low_i)
    low_j = jnp.where(first, -low_i, low_r)
    part = (along(shape, 0).astype(F32) + 0.5) * (two_pi / pixels)
    scale = 1.0 / math.sqrt(pixels)
    part_c, part_s = jnp.cos(part) * (0.375 * scale), jnp.sin(part) * (0.375 * scale)

    @pl.loop(0, count)
    def _(h):
        row = pl.ds(h, 1)
        taper = 0.625 * scale - (high_c[row] * part_c - high_s[row] * part_s)
        value = (high_r[row] * low + high_i[row] * low_j) * taper
        cols_ref[pl.ds(pl.multiple_of(h * block, block), block)] = value.astype(BF16)


def fill_rows(tab_ref, offsets, base_r, base_i, first_row, pixels):
    count = base_r.shape[1]
    subgrids = base_r.shape[0]
    spacing = SKY // pixels
    shape = (CS, count)
    place = first_row + along(shape, 1)
    step_r, step_i = unit(spacing * along(shape, 0) * place % SKY, SKY)
    curve = jnp.sin(math.pi * (place.astype(F32) + 0.5) / pixels)
    scale = (0.25 + 0.75 * curve * curve) / math.sqrt(pixels)
    step_r, step_i = step_r * scale, step_i * scale
    base_r[...], base_i[...] = unit(
        offsets * (first_row + along((subgrids, count), 1)) % SKY, SKY
    )

    @pl.loop(0, subgrids)
    def _(s):
        br, bi = base_r[pl.ds(s, 1)], base_i[pl.ds(s, 1)]
        value = jnp.concatenate(
            [br * step_r - bi * step_i, br * step_i + bi * step_r], axis=1
        )
        tab_ref[pl.ds(pl.multiple_of(s * CS, CS), CS)] = value.astype(BF16)


def grid_tables():
    ratio = SG // CS
    order = (ratio * iota(CS)[None, :] + iota(ratio)[:, None]).reshape(SG)
    cosine, sine = unit(iota(SG)[:, None] * order[None, :] % SG, SG, 1.0)
    real = (cosine / math.sqrt(SG)).astype(BF16)
    imag = (sine / math.sqrt(SG)).astype(BF16)
    left = jnp.concatenate([real, imag], axis=1)
    back = jnp.concatenate([real.T, imag.T], axis=1)
    tr = real.T.reshape(ratio, CS, SG)
    ti = imag.T.reshape(ratio, CS, SG)
    right = jnp.stack(
        [jnp.concatenate([tr, ti], axis=2), jnp.concatenate([-ti, tr], axis=2)], axis=1
    ).reshape(2 * SG, 2 * SG)
    return left, back, right, right.T


def times_i(value):
    half = value.shape[-1] // 2
    return jnp.concatenate([-value[..., half:], value[..., :half]], axis=-1)


def dot(left, right):
    return jnp.dot(left, right, preferred_element_type=F32)


def subgrid_cycle(offset_mod, spacing, rows, count, contrib, left, back, right, right_t, observe, emit):
    ratio = SG // CS
    slot = lax.broadcasted_iota(jnp.int32, (SG, 1), 0) // CS
    angle = (offset_mod * slot % spacing).astype(F32) * (-two_pi / spacing)
    turn_r, turn_i = jnp.cos(angle), jnp.sin(angle)
    fronts = []
    for t in range(TERMS):
        parts = []
        for b in range(ratio):
            raw = contrib(t, b)
            placed = (turn_r * raw + turn_i * times_i(raw)).astype(BF16)
            parts.append(jnp.concatenate([placed, times_i(placed)], axis=0))
        fronts.append(dot(left, jnp.concatenate(parts, axis=1)).astype(BF16))
    sky = [dot(front, right).astype(BF16) for front in fronts]
    tiles = len(rows)
    height = 8
    group = tiles * height
    line = lax.broadcasted_iota(jnp.int32, (group, 1), 0)
    target = jnp.zeros((group, 1), jnp.int32)
    for j in range(tiles):
        target = jnp.where(line // height == j, rows[j] + line - j * height, target)
    live = line // height < count
    column = lax.broadcasted_iota(jnp.int32, (group, SG), 1)
    placer = jnp.where((target == column) & live, 1.0, 0.0).astype(BF16)
    model = [dot(placer, term) for term in sky]
    live_f = live.astype(F32)
    sums = [[], []]
    for j in range(tiles):
        part = slice(j * height, (j + 1) * height)
        sums_j = observe(j, model[0][part], model[1][part], live_f[part])
        sums[0].append(sums_j[0])
        sums[1].append(sums_j[1])
    out = []
    for t in range(TERMS):
        weighted = jnp.concatenate(sums[t], axis=0).astype(BF16)
        regrid = lax.dot_general(
            placer, weighted, (((0,), (0,)), ((), ())), preferred_element_type=F32
        ).astype(BF16)
        front = dot(back, jnp.concatenate([regrid, -times_i(regrid)], axis=0)).astype(BF16)
        grid = dot(front, right_t).astype(BF16).astype(F32)
        out.append([])
        for b in range(ratio):
            part = grid[:, b * SG : (b + 1) * SG]
            out[t].append((turn_r * part - turn_i * times_i(part)).astype(BF16))
    return out


def observe_tile(vis_ref, res_ref, j, first, second, live):
    channels = vis_ref.shape[1]
    sum0 = jnp.zeros(first.shape, F32)
    sum1 = jnp.zeros(first.shape, F32)
    for c in range(channels):
        nu = (c + 0.5) / channels - 0.5
        residual = (vis_ref[j, c].astype(F32) - (first + nu * second)) * live
        res_ref[j, c] = residual.astype(BF16)
        sum0 += residual
        sum1 += nu * residual
    return sum0, sum1


def cycle_kernel(
    pixels, offset_ref, count_ref, place_ref, list_ref, fm_ref,
    left_ref, back_ref, right_ref, right_t_ref, vis_ref,
    strip_ref, res_ref, cols_ref,
    x_ref, g_ref, core_sum, row_recv, row_sum, z_recv, full, turned, back_full,
    buffer, both, tab, high_r, high_i, high_c, high_s, base_r, base_i, total_ref,
    fetch, send, recv,
):
    spacing = SKY // pixels
    chunks, depth, cores, rows, span, lanes = x_ref.shape
    pairs = full.shape[1]
    ratio = SG // CS
    facet, row, sub = lax.axis_index("facet"), lax.axis_index("row"), lax.axis_index("sub")
    core, z = lax.rem(facet, cores), facet // cores
    other = {"facet": facet + 1 - 2 * core}

    def row_peer(d):
        return {"row": lax.rem(row + d, rows)}

    def z_place(d):
        return lax.rem(z + d, depth)

    def z_peer(d):
        return {"facet": z_place(d) * cores + core}

    def sub_place(d):
        return lax.rem(sub + d, pairs)

    def sub_peer(d):
        return {"sub": sub_place(d)}

    peers = [other]
    peers += [row_peer(d) for d in range(1, rows)]
    peers += [z_peer(d) for d in range(1, depth)]
    peers += [sub_peer(d) for d in range(1, pairs)]
    slots, tile = buffer.shape[:2]
    rows_here = both.shape[0] // 2
    tiles_each = rows_here // tile
    steps = chunks * tiles_each

    def load(step):
        slot = lax.rem(step, slots)
        return pltpu.make_async_copy(
            fm_ref.at[pl.ds(pl.multiple_of(step * tile, tile), tile)],
            buffer.at[slot],
            fetch.at[slot],
        )

    for step in range(min(slots, steps)):
        load(step).start()
    barrier = pltpu.get_barrier_semaphore()
    for peer in peers:
        pl.semaphore_signal(barrier, inc=1, device_id=peer, device_id_type=pl.DeviceIdType.MESH)
    fill_columns(cols_ref, high_r, high_i, high_c, high_s)
    pl.semaphore_wait(barrier, len(peers))

    row_at, z_at, sub_at = 1, rows, rows + depth - 1
    started = []

    def send_to(way, chunk, slot, source, target, peer):
        copy = pltpu.make_async_remote_copy(
            src_ref=source,
            dst_ref=target,
            send_sem=send.at[way, chunk, slot],
            recv_sem=recv.at[way, chunk, slot],
            device_id=peer,
            device_id_type=pl.DeviceIdType.MESH,
        )
        copy.start()
        started.append(copy)
        return copy

    def core_start(c):
        @pl.loop(0, tiles_each)
        def _(i):
            step = c * tiles_each + i
            load(step).wait()
            strip = jnp.dot(
                buffer[lax.rem(step, slots)], cols_ref[...], preferred_element_type=F32
            )
            at = pl.multiple_of(i * tile, tile)
            both[pl.ds(at, tile)] = strip.astype(BF16)
            both[pl.ds(rows_here + at, tile)] = times_i(strip).astype(BF16)

            @pl.when(step + slots < steps)
            def _():
                load(step + slots).start()

        if c == 0:
            fill_rows(
                tab, list_ref[...], base_r, base_i,
                (facet * rows + row) * rows_here, pixels,
            )

        @pl.loop(0, depth * cores)
        def _(i):
            at = i * rows * span
            value = dot(tab[pl.ds(pl.multiple_of(at, rows * span), rows * span)], both[...])
            x_ref[c, i // cores, lax.rem(i, cores)] = value.astype(BF16).reshape(
                rows, span, lanes
            )

        return [send_to(0, c, 0, x_ref.at[c, :, 1 - core], core_sum.at[c], other)]

    def row_start(c):
        @pl.loop(0, rows * depth)
        def _(i):
            p, r = i // rows, lax.rem(i, rows)
            total = core_sum[c, p, r].astype(F32) + x_ref[c, p, core, r].astype(F32)
            core_sum[c, p, r] = total.astype(BF16)

        return [
            send_to(
                0, c, row_at + d - 1,
                core_sum.at[c, :, lax.rem(row + d, rows)], row_recv.at[c, d - 1], row_peer(d),
            )
            for d in range(1, rows)
        ]

    def z_start(c):
        @pl.loop(0, depth)
        def _(p):
            total = core_sum[c, p, row].astype(F32)
            for d in range(1, rows):
                total += row_recv[c, d - 1, p].astype(F32)
            row_sum[c, p] = total.astype(BF16)

        return [
            send_to(
                0, c, z_at + d - 1, row_sum.at[c, z_place(d)], z_recv.at[c, d - 1], z_peer(d)
            )
            for d in range(1, depth)
        ]

    def sub_start(c):
        total = row_sum[c, z].astype(F32)
        for d in range(1, depth):
            total += z_recv[c, d - 1].astype(F32)
        z_recv[c, 0] = total.astype(BF16)
        full[c, sub] = z_recv[c, 0, pl.ds(pl.multiple_of(sub * CS, CS), CS)]
        return [
            send_to(
                0, c, sub_at + d - 1,
                z_recv.at[c, 0, pl.ds(pl.multiple_of(sub_place(d) * CS, CS), CS)],
                full.at[c, sub], sub_peer(d),
            )
            for d in range(1, pairs)
        ]

    def wait(copies):
        for copy in copies:
            copy.wait_recv()

    def run(stages):
        flying = [[None] * chunks for _ in stages]
        for step in range(chunks + len(stages) - 1):
            for level in range(len(stages) - 1, -1, -1):
                c = step - level
                if 0 <= c < chunks:
                    if level:
                        wait(flying[level - 1][c])
                    flying[level][c] = stages[level](c)
        for c in range(chunks):
            wait(flying[-1][c])

    run([core_start, row_start, z_start, sub_start])

    tiles = vis_ref.shape[0]

    def contrib(t, b):
        return jnp.concatenate(
            [full[t * ratio + a, b].astype(F32) for a in range(ratio)], axis=0
        )

    owner = (facet * rows + row) * pairs + sub
    out = subgrid_cycle(
        lax.rem(offset_ref[owner], spacing), spacing, [place_ref[0, j] for j in range(tiles)],
        count_ref[0], contrib,
        left_ref[...], back_ref[...], right_ref[...], right_t_ref[...],
        functools.partial(observe_tile, vis_ref, res_ref), None,
    )
    for t in range(TERMS):
        for b in range(ratio):
            for a in range(ratio):
                turned[t * ratio + a, b] = out[t][b][a * CS : (a + 1) * CS]

    def back_sub(c):
        back_full[c, sub] = turned[c, sub]
        return [
            send_to(1, c, sub_at + d - 1, turned.at[c, sub_place(d)], back_full.at[c, sub], sub_peer(d))
            for d in range(1, pairs)
        ]

    def back_z(c):
        block = jnp.concatenate([back_full[c, q].astype(F32) for q in range(pairs)], axis=0)
        g_ref[c, z, core, row] = block.T.astype(BF16)
        mine = g_ref.at[c, z, core, row]
        return [send_to(1, c, z_at + d - 1, mine, mine, z_peer(d)) for d in range(1, depth)]

    def back_row(c):
        mine = g_ref.at[c, :, core, row]
        return [send_to(1, c, row_at + d - 1, mine, mine, row_peer(d)) for d in range(1, rows)]

    def back_core(c):
        mine = g_ref.at[c, :, core]
        return [send_to(1, c, 0, mine, mine, other)]

    run([back_sub, back_z, back_row, back_core])

    total_ref[...] = jnp.zeros_like(total_ref)

    @pl.loop(0, depth * cores * rows)
    def _(i):
        p, h, r = i // (cores * rows), lax.rem(i // rows, cores), lax.rem(i, rows)
        block = jnp.concatenate([g_ref[c, p, h, r] for c in range(chunks)], axis=0)
        halves = [block[q * CS : (q + 1) * CS] for q in range(2 * chunks)]
        swapped = []
        for c in range(chunks):
            swapped += [halves[2 * c + 1], -halves[2 * c]]
        rows_at = tab[pl.ds(pl.multiple_of(i * span, span), span)]
        total_ref[...] += dot(block, rows_at[:, :rows_here]) + dot(
            jnp.concatenate(swapped, axis=0), rows_at[:, rows_here:]
        )

    for c in range(chunks):
        strip_ref[c] = total_ref[c * lanes : (c + 1) * lanes].T.astype(BF16)
    for copy in started:
        copy.wait_send()


def exchange(facet_rows, sub_offsets, tile_counts, tile_rows, tables, observed, chunks, dims):
    rows, depth, pairs = dims
    cores = 2
    pixels = facet_rows.shape[1]
    rows_here = facet_rows.shape[0] // chunks
    subgrids = sub_offsets.shape[0]
    span, lanes = pairs * CS, 2 * CS
    tile = math.gcd(rows_here, 256)
    vmem = pl.BlockSpec(memory_space=pltpu.VMEM)
    smem = pl.BlockSpec(memory_space=pltpu.SMEM)
    slots = rows + depth + pairs - 2
    whole = (chunks, depth, cores, rows, span, lanes)
    return pl.pallas_call(
        functools.partial(cycle_kernel, pixels),
        out_shape=(
            jax.ShapeDtypeStruct((chunks, rows_here, lanes), BF16),
            jax.ShapeDtypeStruct(observed.shape, BF16),
            jax.ShapeDtypeStruct((pixels, lanes), BF16),
        ),
        in_specs=[smem] * 3 + [vmem, pl.BlockSpec(memory_space=pl.ANY)] + [vmem] * 5,
        out_specs=(vmem, vmem, vmem),
        scratch_shapes=[
            pltpu.VMEM(whole, BF16),
            pltpu.VMEM((*whole[:4], lanes, span), BF16),
            pltpu.VMEM((chunks, depth, rows, span, lanes), BF16),
            pltpu.VMEM((chunks, rows - 1, depth, span, lanes), BF16),
            pltpu.VMEM((chunks, depth, span, lanes), BF16),
            pltpu.VMEM((chunks, depth - 1, span, lanes), BF16),
            pltpu.VMEM((chunks, pairs, CS, lanes), BF16),
            pltpu.VMEM((chunks, pairs, CS, lanes), BF16),
            pltpu.VMEM((chunks, pairs, CS, lanes), BF16),
            pltpu.VMEM((3, tile, pixels), BF16),
            pltpu.VMEM((2 * rows_here, lanes), BF16),
            pltpu.VMEM((subgrids * CS, 2 * rows_here), BF16),
            pltpu.VMEM((pixels // 128, lanes), F32),
            pltpu.VMEM((pixels // 128, lanes), F32),
            pltpu.VMEM((pixels // 128, lanes), F32),
            pltpu.VMEM((pixels // 128, lanes), F32),
            pltpu.VMEM((subgrids, rows_here), F32),
            pltpu.VMEM((subgrids, rows_here), F32),
            pltpu.VMEM((chunks * lanes, rows_here), F32),
            pltpu.SemaphoreType.DMA((3,)),
            pltpu.SemaphoreType.DMA((2, chunks, slots)),
            pltpu.SemaphoreType.DMA((2, chunks, slots)),
        ],
        compiler_params=pltpu.CompilerParams(
            collective_id=0, has_side_effects=True, vmem_limit_bytes=VMEM_LIMIT
        ),
    )(
        sub_offsets, tile_counts, tile_rows, sub_offsets.reshape(subgrids, 1),
        facet_rows, *tables, observed,
    )


def spread_kernel(strip_ref, cols_ref, out_ref):
    pixels = cols_ref.shape[0]
    block = 1024

    @pl.loop(0, pixels // block)
    def _(i):
        at = pl.ds(pl.multiple_of(i * block, block), block)
        out_ref[:, at] = lax.dot_general(
            strip_ref[...], cols_ref[at], (((1,), (1,)), ((), ())), preferred_element_type=F32
        ).astype(BF16)


def spread(strips, columns):
    count, lanes = strips.shape
    pixels = columns.shape[0]
    tile = math.gcd(count, 256)
    return pl.pallas_call(
        spread_kernel,
        grid=(count // tile,),
        out_shape=jax.ShapeDtypeStruct((count, pixels), BF16),
        in_specs=[
            pl.BlockSpec((tile, lanes), lambda i: (i, 0)),
            pl.BlockSpec((pixels, lanes), lambda i: (0, 0)),
        ],
        out_specs=pl.BlockSpec((tile, pixels), lambda i: (i, 0)),
        compiler_params=pltpu.CompilerParams(vmem_limit_bytes=32 * 2**20),
    )(strips, columns)


def local(facet_model, sub_offsets, tile_rows, tile_counts, visibilities):
    terms, facets, rows_here, pixels = facet_model.shape
    chunks = terms * facets
    dims = (lax.axis_size("row"), lax.axis_size("facet") // 2, lax.axis_size("sub"))
    strips, residual, columns = exchange(
        facet_model.reshape(chunks * rows_here, pixels), sub_offsets, tile_counts, tile_rows,
        grid_tables(), visibilities[0], chunks, dims,
    )
    residual_facets = spread(strips.reshape(chunks * rows_here, 2 * CS), columns)
    return (residual_facets.reshape(facet_model.shape), residual[None])


def solution(mesh):
    placed = (
        P(None, "sub", ("facet", "row"), None),
        P(),
        P(("facet", "row", "sub"), None),
        P(("facet", "row", "sub")),
        P(("facet", "row", "sub"), None, None, None, None),
    )
    return jax.shard_map(
        local,
        mesh=mesh,
        in_specs=placed,
        out_specs=(
            P(None, "sub", ("facet", "row"), None),
            P(("facet", "row", "sub"), None, None, None, None),
        ),
        check_vma=False,
    )
```

```python
import functools
import math

import jax
import jax.numpy as jnp
from jax import lax
from jax.experimental import pallas as pl
from jax.experimental.pallas import tpu as pltpu
from jax.sharding import PartitionSpec as P

SKY = 65536
CS = 64
SG = 128
TERMS = 2
VMEM_LIMIT = 62 * 2**20

two_pi = 2.0 * math.pi
F32 = jnp.float32
BF16 = jnp.bfloat16


def unit(phase, modulus, sign=-1.0):
    angle = phase.astype(F32) * (sign * two_pi / modulus)
    return jnp.cos(angle), jnp.sin(angle)


def iota(count):
    return jnp.arange(count, dtype=jnp.int32)


def along(shape, axis):
    return lax.broadcasted_iota(jnp.int32, shape, axis)


def fill_columns(cols_ref, high_r, high_i, high_c, high_s):
    pixels, lanes = cols_ref.shape
    spacing = SKY // pixels
    block = 128
    count = pixels // block
    freq = spacing * lax.rem(along((count, lanes), 1), CS)
    high_r[...], high_i[...] = unit(freq * (block * along((count, lanes), 0)) % SKY, SKY)
    step = block * along((count, lanes), 0).astype(F32) * (two_pi / pixels)
    high_c[...], high_s[...] = jnp.cos(step), jnp.sin(step)
    shape = (block, lanes)
    low_r, low_i = unit(spacing * lax.rem(along(shape, 1), CS) * along(shape, 0) % SKY, SKY)
    first = along(shape, 1) < CS
    low = jnp.where(first, low_r, low_i)
    low_j = jnp.where(first, -low_i, low_r)
    part = (along(shape, 0).astype(F32) + 0.5) * (two_pi / pixels)
    scale = 1.0 / math.sqrt(pixels)
    part_c, part_s = jnp.cos(part) * (0.375 * scale), jnp.sin(part) * (0.375 * scale)

    @pl.loop(0, count)
    def _(h):
        row = pl.ds(h, 1)
        taper = 0.625 * scale - (high_c[row] * part_c - high_s[row] * part_s)
        value = (high_r[row] * low + high_i[row] * low_j) * taper
        cols_ref[pl.ds(pl.multiple_of(h * block, block), block)] = value.astype(BF16)


def fill_rows(tab_ref, offsets, base_r, base_i, first_row, pixels):
    count = base_r.shape[1]
    subgrids = base_r.shape[0]
    spacing = SKY // pixels
    shape = (CS, count)
    place = first_row + along(shape, 1)
    step_r, step_i = unit(spacing * along(shape, 0) * place % SKY, SKY)
    curve = jnp.sin(math.pi * (place.astype(F32) + 0.5) / pixels)
    scale = (0.25 + 0.75 * curve * curve) / math.sqrt(pixels)
    step_r, step_i = step_r * scale, step_i * scale
    base_r[...], base_i[...] = unit(
        offsets * (first_row + along((subgrids, count), 1)) % SKY, SKY
    )

    @pl.loop(0, subgrids)
    def _(s):
        br, bi = base_r[pl.ds(s, 1)], base_i[pl.ds(s, 1)]
        value = jnp.concatenate(
            [br * step_r - bi * step_i, br * step_i + bi * step_r], axis=1
        )
        tab_ref[pl.ds(pl.multiple_of(s * CS, CS), CS)] = value.astype(BF16)


def grid_tables():
    ratio = SG // CS
    order = (ratio * iota(CS)[None, :] + iota(ratio)[:, None]).reshape(SG)
    cosine, sine = unit(iota(SG)[:, None] * order[None, :] % SG, SG, 1.0)
    real = (cosine / math.sqrt(SG)).astype(BF16)
    imag = (sine / math.sqrt(SG)).astype(BF16)
    left = jnp.concatenate([real, imag], axis=1)
    back = jnp.concatenate([real.T, imag.T], axis=1)
    tr = real.T.reshape(ratio, CS, SG)
    ti = imag.T.reshape(ratio, CS, SG)
    right = jnp.stack(
        [jnp.concatenate([tr, ti], axis=2), jnp.concatenate([-ti, tr], axis=2)], axis=1
    ).reshape(2 * SG, 2 * SG)
    return left, back, right, right.T


def times_i(value):
    half = value.shape[-1] // 2
    return jnp.concatenate([-value[..., half:], value[..., :half]], axis=-1)


def dot(left, right):
    return jnp.dot(left, right, preferred_element_type=F32)


def subgrid_cycle(offset_mod, spacing, rows, count, contrib, left, back, right, right_t, observe, emit):
    ratio = SG // CS
    slot = lax.broadcasted_iota(jnp.int32, (SG, 1), 0) // CS
    angle = (offset_mod * slot % spacing).astype(F32) * (-two_pi / spacing)
    turn_r, turn_i = jnp.cos(angle), jnp.sin(angle)
    fronts = []
    for t in range(TERMS):
        parts = []
        for b in range(ratio):
            raw = contrib(t, b)
            placed = (turn_r * raw + turn_i * times_i(raw)).astype(BF16)
            parts.append(jnp.concatenate([placed, times_i(placed)], axis=0))
        fronts.append(dot(left, jnp.concatenate(parts, axis=1)).astype(BF16))
    sky = [dot(front, right).astype(BF16) for front in fronts]
    tiles = len(rows)
    height = 8
    group = tiles * height
    line = lax.broadcasted_iota(jnp.int32, (group, 1), 0)
    target = jnp.zeros((group, 1), jnp.int32)
    for j in range(tiles):
        target = jnp.where(line // height == j, rows[j] + line - j * height, target)
    live = line // height < count
    column = lax.broadcasted_iota(jnp.int32, (group, SG), 1)
    placer = jnp.where((target == column) & live, 1.0, 0.0).astype(BF16)
    model = [dot(placer, term) for term in sky]
    live_f = live.astype(F32)
    sums = [[], []]
    for j in range(tiles):
        part = slice(j * height, (j + 1) * height)
        sums_j = observe(j, model[0][part], model[1][part], live_f[part])
        sums[0].append(sums_j[0])
        sums[1].append(sums_j[1])
    out = []
    for t in range(TERMS):
        weighted = jnp.concatenate(sums[t], axis=0).astype(BF16)
        regrid = lax.dot_general(
            placer, weighted, (((0,), (0,)), ((), ())), preferred_element_type=F32
        ).astype(BF16)
        front = dot(back, jnp.concatenate([regrid, -times_i(regrid)], axis=0)).astype(BF16)
        grid = dot(front, right_t).astype(BF16).astype(F32)
        out.append([])
        for b in range(ratio):
            part = grid[:, b * SG : (b + 1) * SG]
            out[t].append((turn_r * part - turn_i * times_i(part)).astype(BF16))
    return out


def observe_tile(vis_ref, res_ref, j, first, second, live):
    channels = vis_ref.shape[1]
    sum0 = jnp.zeros(first.shape, F32)
    sum1 = jnp.zeros(first.shape, F32)
    for c in range(channels):
        nu = (c + 0.5) / channels - 0.5
        residual = (vis_ref[j, c].astype(F32) - (first + nu * second)) * live
        res_ref[j, c] = residual.astype(BF16)
        sum0 += residual
        sum1 += nu * residual
    return sum0, sum1


def cycle_kernel(
    pixels, offset_ref, count_ref, place_ref, list_ref, fm_ref,
    left_ref, back_ref, right_ref, right_t_ref, vis_ref,
    strip_ref, res_ref, cols_ref,
    x_ref, g_ref, core_sum, row_recv, row_sum, z_recv, full, turned, back_full,
    buffer, both, tab, high_r, high_i, high_c, high_s, base_r, base_i, total_ref,
    fetch, send, recv,
):
    spacing = SKY // pixels
    chunks, depth, cores, rows, span, lanes = x_ref.shape
    pairs = full.shape[1]
    ratio = SG // CS
    facet, row, sub = lax.axis_index("facet"), lax.axis_index("row"), lax.axis_index("sub")
    core, z = lax.rem(facet, cores), facet // cores
    other = {"facet": facet + 1 - 2 * core}

    def row_peer(d):
        return {"row": lax.rem(row + d, rows)}

    def z_place(d):
        return lax.rem(z + d, depth)

    def z_peer(d):
        return {"facet": z_place(d) * cores + core}

    def sub_place(d):
        return lax.rem(sub + d, pairs)

    def sub_peer(d):
        return {"sub": sub_place(d)}

    peers = [other]
    peers += [row_peer(d) for d in range(1, rows)]
    peers += [z_peer(d) for d in range(1, depth)]
    peers += [sub_peer(d) for d in range(1, pairs)]
    slots, tile = buffer.shape[:2]
    rows_here = both.shape[0] // 2
    tiles_each = rows_here // tile
    steps = chunks * tiles_each

    def load(step):
        slot = lax.rem(step, slots)
        return pltpu.make_async_copy(
            fm_ref.at[pl.ds(pl.multiple_of(step * tile, tile), tile)],
            buffer.at[slot],
            fetch.at[slot],
        )

    for step in range(min(slots, steps)):
        load(step).start()
    barrier = pltpu.get_barrier_semaphore()
    for peer in peers:
        pl.semaphore_signal(barrier, inc=1, device_id=peer, device_id_type=pl.DeviceIdType.MESH)
    fill_columns(cols_ref, high_r, high_i, high_c, high_s)
    pl.semaphore_wait(barrier, len(peers))

    row_at, z_at, sub_at = 1, rows, rows + depth - 1
    started = []

    def send_to(way, chunk, slot, source, target, peer):
        copy = pltpu.make_async_remote_copy(
            src_ref=source,
            dst_ref=target,
            send_sem=send.at[way, chunk, slot],
            recv_sem=recv.at[way, chunk, slot],
            device_id=peer,
            device_id_type=pl.DeviceIdType.MESH,
        )
        copy.start()
        started.append(copy)
        return copy

    def core_start(c):
        @pl.loop(0, tiles_each)
        def _(i):
            step = c * tiles_each + i
            load(step).wait()
            strip = jnp.dot(
                buffer[lax.rem(step, slots)], cols_ref[...], preferred_element_type=F32
            )
            at = pl.multiple_of(i * tile, tile)
            both[pl.ds(at, tile)] = strip.astype(BF16)
            both[pl.ds(rows_here + at, tile)] = times_i(strip).astype(BF16)

            @pl.when(step + slots < steps)
            def _():
                load(step + slots).start()

        if c == 0:
            fill_rows(
                tab, list_ref[...], base_r, base_i,
                (facet * rows + row) * rows_here, pixels,
            )

        @pl.loop(0, depth * cores)
        def _(i):
            at = i * rows * span
            value = dot(tab[pl.ds(pl.multiple_of(at, rows * span), rows * span)], both[...])
            x_ref[c, i // cores, lax.rem(i, cores)] = value.astype(BF16).reshape(
                rows, span, lanes
            )

        return [send_to(0, c, 0, x_ref.at[c, :, 1 - core], core_sum.at[c], other)]

    def row_start(c):
        @pl.loop(0, rows * depth)
        def _(i):
            p, r = i // rows, lax.rem(i, rows)
            total = core_sum[c, p, r].astype(F32) + x_ref[c, p, core, r].astype(F32)
            core_sum[c, p, r] = total.astype(BF16)

        return [
            send_to(
                0, c, row_at + d - 1,
                core_sum.at[c, :, lax.rem(row + d, rows)], row_recv.at[c, d - 1], row_peer(d),
            )
            for d in range(1, rows)
        ]

    def z_start(c):
        @pl.loop(0, depth)
        def _(p):
            total = core_sum[c, p, row].astype(F32)
            for d in range(1, rows):
                total += row_recv[c, d - 1, p].astype(F32)
            row_sum[c, p] = total.astype(BF16)

        return [
            send_to(
                0, c, z_at + d - 1, row_sum.at[c, z_place(d)], z_recv.at[c, d - 1], z_peer(d)
            )
            for d in range(1, depth)
        ]

    def sub_start(c):
        total = row_sum[c, z].astype(F32)
        for d in range(1, depth):
            total += z_recv[c, d - 1].astype(F32)
        z_recv[c, 0] = total.astype(BF16)
        full[c, sub] = z_recv[c, 0, pl.ds(pl.multiple_of(sub * CS, CS), CS)]
        return [
            send_to(
                0, c, sub_at + d - 1,
                z_recv.at[c, 0, pl.ds(pl.multiple_of(sub_place(d) * CS, CS), CS)],
                full.at[c, sub], sub_peer(d),
            )
            for d in range(1, pairs)
        ]

    def wait(copies):
        for copy in copies:
            copy.wait_recv()

    def run(stages, lead):
        flying = [[None] * chunks for _ in stages]
        order = sorted(
            (c + sum(lead[:level]), -level, level, c)
            for level in range(len(stages))
            for c in range(chunks)
        )
        for _, _, level, c in order:
            if level:
                wait(flying[level - 1][c])
            flying[level][c] = stages[level](c)
        for c in range(chunks):
            wait(flying[-1][c])

    run([core_start, row_start, z_start, sub_start], [1, chunks - 1, chunks - 1])

    tiles = vis_ref.shape[0]

    def contrib(t, b):
        return jnp.concatenate(
            [full[t * ratio + a, b].astype(F32) for a in range(ratio)], axis=0
        )

    owner = (facet * rows + row) * pairs + sub
    out = subgrid_cycle(
        lax.rem(offset_ref[owner], spacing), spacing, [place_ref[0, j] for j in range(tiles)],
        count_ref[0], contrib,
        left_ref[...], back_ref[...], right_ref[...], right_t_ref[...],
        functools.partial(observe_tile, vis_ref, res_ref), None,
    )
    for t in range(TERMS):
        for b in range(ratio):
            for a in range(ratio):
                turned[t * ratio + a, b] = out[t][b][a * CS : (a + 1) * CS]

    def back_sub(c):
        back_full[c, sub] = turned[c, sub]
        return [
            send_to(1, c, sub_at + d - 1, turned.at[c, sub_place(d)], back_full.at[c, sub], sub_peer(d))
            for d in range(1, pairs)
        ]

    def back_z(c):
        block = jnp.concatenate([back_full[c, q].astype(F32) for q in range(pairs)], axis=0)
        g_ref[c, z, core, row] = block.T.astype(BF16)
        mine = g_ref.at[c, z, core, row]
        return [send_to(1, c, z_at + d - 1, mine, mine, z_peer(d)) for d in range(1, depth)]

    def back_row(c):
        mine = g_ref.at[c, :, core, row]
        return [send_to(1, c, row_at + d - 1, mine, mine, row_peer(d)) for d in range(1, rows)]

    def back_core(c):
        mine = g_ref.at[c, :, core]
        return [send_to(1, c, 0, mine, mine, other)]

    run([back_sub, back_z, back_row, back_core], [chunks - 1, 2, 3])

    total_ref[...] = jnp.zeros_like(total_ref)

    @pl.loop(0, depth * cores * rows)
    def _(i):
        p, h, r = i // (cores * rows), lax.rem(i // rows, cores), lax.rem(i, rows)
        block = jnp.concatenate([g_ref[c, p, h, r] for c in range(chunks)], axis=0)
        halves = [block[q * CS : (q + 1) * CS] for q in range(2 * chunks)]
        swapped = []
        for c in range(chunks):
            swapped += [halves[2 * c + 1], -halves[2 * c]]
        rows_at = tab[pl.ds(pl.multiple_of(i * span, span), span)]
        total_ref[...] += dot(block, rows_at[:, :rows_here]) + dot(
            jnp.concatenate(swapped, axis=0), rows_at[:, rows_here:]
        )

    for c in range(chunks):
        strip_ref[c] = total_ref[c * lanes : (c + 1) * lanes].T.astype(BF16)
    for copy in started:
        copy.wait_send()


def exchange(facet_rows, sub_offsets, tile_counts, tile_rows, tables, observed, chunks, dims):
    rows, depth, pairs = dims
    cores = 2
    pixels = facet_rows.shape[1]
    rows_here = facet_rows.shape[0] // chunks
    subgrids = sub_offsets.shape[0]
    span, lanes = pairs * CS, 2 * CS
    tile = math.gcd(rows_here, 256)
    vmem = pl.BlockSpec(memory_space=pltpu.VMEM)
    smem = pl.BlockSpec(memory_space=pltpu.SMEM)
    slots = rows + depth + pairs - 2
    whole = (chunks, depth, cores, rows, span, lanes)
    return pl.pallas_call(
        functools.partial(cycle_kernel, pixels),
        out_shape=(
            jax.ShapeDtypeStruct((chunks, rows_here, lanes), BF16),
            jax.ShapeDtypeStruct(observed.shape, BF16),
            jax.ShapeDtypeStruct((pixels, lanes), BF16),
        ),
        in_specs=[smem] * 3 + [vmem, pl.BlockSpec(memory_space=pl.ANY)] + [vmem] * 5,
        out_specs=(vmem, vmem, vmem),
        scratch_shapes=[
            pltpu.VMEM(whole, BF16),
            pltpu.VMEM((*whole[:4], lanes, span), BF16),
            pltpu.VMEM((chunks, depth, rows, span, lanes), BF16),
            pltpu.VMEM((chunks, rows - 1, depth, span, lanes), BF16),
            pltpu.VMEM((chunks, depth, span, lanes), BF16),
            pltpu.VMEM((chunks, depth - 1, span, lanes), BF16),
            pltpu.VMEM((chunks, pairs, CS, lanes), BF16),
            pltpu.VMEM((chunks, pairs, CS, lanes), BF16),
            pltpu.VMEM((chunks, pairs, CS, lanes), BF16),
            pltpu.VMEM((3, tile, pixels), BF16),
            pltpu.VMEM((2 * rows_here, lanes), BF16),
            pltpu.VMEM((subgrids * CS, 2 * rows_here), BF16),
            pltpu.VMEM((pixels // 128, lanes), F32),
            pltpu.VMEM((pixels // 128, lanes), F32),
            pltpu.VMEM((pixels // 128, lanes), F32),
            pltpu.VMEM((pixels // 128, lanes), F32),
            pltpu.VMEM((subgrids, rows_here), F32),
            pltpu.VMEM((subgrids, rows_here), F32),
            pltpu.VMEM((chunks * lanes, rows_here), F32),
            pltpu.SemaphoreType.DMA((3,)),
            pltpu.SemaphoreType.DMA((2, chunks, slots)),
            pltpu.SemaphoreType.DMA((2, chunks, slots)),
        ],
        compiler_params=pltpu.CompilerParams(
            collective_id=0, has_side_effects=True, vmem_limit_bytes=VMEM_LIMIT
        ),
    )(
        sub_offsets, tile_counts, tile_rows, sub_offsets.reshape(subgrids, 1),
        facet_rows, *tables, observed,
    )


def spread_kernel(strip_ref, cols_ref, out_ref, turned_ref):
    turned_ref[...] = cols_ref[...].astype(F32).T.astype(BF16)
    count = strip_ref.shape[0]
    block = math.gcd(count, 256)

    @pl.loop(0, count // block)
    def _(i):
        at = pl.ds(pl.multiple_of(i * block, block), block)
        out_ref[at] = dot(strip_ref[at], turned_ref[...]).astype(BF16)


def spread(strips, columns):
    count, lanes = strips.shape
    pixels = columns.shape[0]
    block = math.gcd(pixels, 1024)
    return pl.pallas_call(
        spread_kernel,
        grid=(pixels // block,),
        out_shape=jax.ShapeDtypeStruct((count, pixels), BF16),
        in_specs=[
            pl.BlockSpec((count, lanes), lambda i: (0, 0)),
            pl.BlockSpec((block, lanes), lambda i: (i, 0)),
        ],
        out_specs=pl.BlockSpec((count, block), lambda i: (0, i)),
        scratch_shapes=[pltpu.VMEM((lanes, block), BF16)],
        compiler_params=pltpu.CompilerParams(vmem_limit_bytes=32 * 2**20),
    )(strips, columns)


def local(facet_model, sub_offsets, tile_rows, tile_counts, visibilities):
    terms, facets, rows_here, pixels = facet_model.shape
    chunks = terms * facets
    dims = (lax.axis_size("row"), lax.axis_size("facet") // 2, lax.axis_size("sub"))
    strips, residual, columns = exchange(
        facet_model.reshape(chunks * rows_here, pixels), sub_offsets, tile_counts, tile_rows,
        grid_tables(), visibilities[0], chunks, dims,
    )
    residual_facets = spread(strips.reshape(chunks * rows_here, 2 * CS), columns)
    return (residual_facets.reshape(facet_model.shape), residual[None])


def solution(mesh):
    placed = (
        P(None, "sub", ("facet", "row"), None),
        P(),
        P(("facet", "row", "sub"), None),
        P(("facet", "row", "sub")),
        P(("facet", "row", "sub"), None, None, None, None),
    )
    return jax.shard_map(
        local,
        mesh=mesh,
        in_specs=placed,
        out_specs=(
            P(None, "sub", ("facet", "row"), None),
            P(("facet", "row", "sub"), None, None, None, None),
        ),
        check_vma=False,
    )
```
